32 devices in a mesh: phases: 2 (over x), tiles: 16 (over z, y, core).
Axes of the slice: x: 2, y: 2, z: 4, core: 2. Of those that a mesh axis runs over, the one named last changes fastest.
Arguments:
- kspace_grid: float32 [4, 32, 2, 64, 384], P('phases', 'tiles'), may hold values from -6 to 6
- samples: float32 [4, 128, 32, 128], P('phases', 'tiles'), may hold values from -6 to 6
- interp_matrix: bfloat16 [4, 16, 64, 384], P('phases', 'tiles'), may hold values from -0.3125 to 0.3125
- kernel_real: bfloat16 [5, 3, 32, 32], replicated, may hold values from -0.1875 to 0.1875
- kernel_imag: bfloat16 [5, 3, 32, 32], replicated, may hold values from -0.1875 to 0.1875
- segment_line: int32 [4, 16, 16, 2], P('phases', 'tiles'), may hold values from 0 to 3, as said below
- segment_readout: int32 [4, 16, 16, 2], P('phases', 'tiles'), may hold values from 0 to 7, as said below
- segment_count: int32 [4, 16, 16], P('phases', 'tiles'), may hold values from 0 to 2, as said below
Outputs:
- gradient: float32 [4, 32, 2, 64, 384], P('phases', 'tiles')
- data_residual: float32 [4, 128, 32, 128], P('phases', 'tiles')
The draws below stay inside these ranges and needn't reach their ends.
Inputs may be any that keep to these rules, and one draw needn't show every extreme that they name: segment_count[p, t, o] slots, numbered from 0, are in use from tile t to owner o in phase p; every tile t with 8 - w <= t < 8 + w, w = max(2, 1), and in each phase one owner from every tile, have all 2 slots in use. `segment_line`: a line l of a tile stands for plane l // 2 and position l % 2 of that tile. `segment_readout`: readouts are numbered within their owner.
All inputs are finite; a program needn't handle non-finite values.
Results may differ from the reference program's by a relative error of at most 0.0029.
Values may be sent and summed in bfloat16 or wider, within the bound.
A program may use at most 64 MiB of HBM per device.

```python
import jax
import jax.numpy as jnp
from jax import lax

COILS = 32
KX = 5
KZ = 3
NY = 2
NZ = 384
SEG = 64
CAP = 2
READ_DEV = 8
TILE_COUNT = 16
PHASES = 4
NX = 32
CH = 64
LINES = 4
READS = 128


def draw_segment_line(key, part):
    shape_all = (PHASES, TILE_COUNT, TILE_COUNT, CAP)
    values = jax.random.randint(jax.random.fold_in(key, 11), shape_all, 0, LINES)
    slot_flat = jnp.arange(TILE_COUNT)[:, None] * CAP + jnp.arange(CAP)[None, :]
    first_pos = jax.random.randint(jax.random.fold_in(key, 12), (PHASES, TILE_COUNT, 1, 1), 0, TILE_COUNT * CAP)
    second_pos = (first_pos + 1) % (TILE_COUNT * CAP)
    values = jnp.where(slot_flat == first_pos, LINES - 1, jnp.where(slot_flat == second_pos, 0, values))
    return values.astype(jnp.int32)


def draw_segment_readout(key, part):
    shape_all = (PHASES, TILE_COUNT, TILE_COUNT, CAP)
    values = jax.random.randint(jax.random.fold_in(key, 21), shape_all, 0, READ_DEV)
    slot_flat = jnp.arange(TILE_COUNT)[:, None, None] * CAP + jnp.arange(CAP)[None, None, :]
    first_pos = jax.random.randint(jax.random.fold_in(key, 22), (PHASES, 1, TILE_COUNT, 1), 0, TILE_COUNT * CAP)
    second_pos = (first_pos + 1) % (TILE_COUNT * CAP)
    values = jnp.where(slot_flat == first_pos, READ_DEV - 1, jnp.where(slot_flat == second_pos, 0, values))
    return values.astype(jnp.int32)


def draw_segment_count(key, part):
    shape_all = (PHASES, TILE_COUNT, TILE_COUNT)
    margin_tiles = max(TILE_COUNT // 8, 1)
    source = jnp.arange(TILE_COUNT)
    center = (source >= TILE_COUNT // 2 - margin_tiles) & (source < TILE_COUNT // 2 + margin_tiles)
    full_owner = jax.random.randint(jax.random.fold_in(key, 31), (PHASES, 1, 1), 0, TILE_COUNT)
    light = jax.random.randint(jax.random.fold_in(key, 32), shape_all, 0, CAP + 1)
    light = light * jax.random.randint(jax.random.fold_in(key, 33), shape_all, 0, 2)
    owner = jnp.arange(TILE_COUNT)[None, None, :]
    filled = center[None, :, None] | (owner == full_owner)
    return jnp.where(filled, CAP, light).astype(jnp.int32)


def shard_levels(own_key, dims, pieces, least, high):
    def one(position, shards_of):
        heights = jax.random.uniform(jax.random.fold_in(jax.random.fold_in(own_key, 6), position), (shards_of,), jnp.float32, least / len(pieces), high / len(pieces))
        return jnp.repeat(jnp.exp(heights), dims[position] // shards_of).reshape((-1,) + (1,) * (len(dims) - position - 1))

    gain = one(*pieces[0])
    for cut in pieces[1:]:
        gain = gain * one(*cut)
    return gain


def bell_draw(key, extent, scale, limit, shards=(), dtype=jnp.bfloat16):
    drawn = jax.random.normal(key, extent, jnp.float32) * scale
    if len(shards) > 0:
        drawn = shard_levels(key, extent, shards, -0.22, 0.18) * drawn
    return jnp.clip(drawn, min=-limit, max=limit).astype(dtype)


def setup_inputs(seed: int = 0) -> dict:
    streams_of = jax.random.split(jax.random.key(seed), 9)
    kspace_grid = bell_draw(streams_of[0], (PHASES, NX, NY, CH, NZ), 1.0, 6.0, ((0, 2), (1, 16)), jnp.float32)
    samples = bell_draw(streams_of[1], (PHASES, READS, COILS, 2 * SEG), 1.0, 6.0, ((0, 2), (1, 16)), jnp.float32)
    interp_matrix = bell_draw(streams_of[2], (PHASES, TILE_COUNT, SEG, NZ), NZ ** -0.5, 0.3125, ((0, 2), (1, 16)))
    kernel_real = bell_draw(streams_of[3], (KX, KZ, COILS, COILS), (2 * KX * KZ * COILS) ** -0.5, 0.1875)
    kernel_imag = bell_draw(streams_of[4], (KX, KZ, COILS, COILS), (2 * KX * KZ * COILS) ** -0.5, 0.1875)
    segment_line = draw_segment_line(jax.random.fold_in(streams_of[8], 71), 0)
    segment_readout = draw_segment_readout(jax.random.fold_in(streams_of[8], 71), 0)
    segment_count = draw_segment_count(jax.random.fold_in(streams_of[8], 71), 0)
    return {"kspace_grid": kspace_grid, "samples": samples, "interp_matrix": interp_matrix, "kernel_real": kernel_real, "kernel_imag": kernel_imag, "segment_line": segment_line, "segment_readout": segment_readout, "segment_count": segment_count}


SPIRIT_WEIGHT = 1.0
PHASE_WEIGHT = 0.15

def real_form(kernel_real, kernel_imag):
    real_part = kernel_real.astype(jnp.float32)
    imag_part = kernel_imag.astype(jnp.float32)
    upper_half = jnp.stack([real_part, -imag_part], axis=-1)
    lower_half = jnp.stack([imag_part, real_part], axis=-1)
    blocks = jnp.stack([upper_half, lower_half], axis=-3)
    block_shape = blocks.shape
    return blocks.reshape(block_shape[0], block_shape[1], block_shape[2] * 2, block_shape[4] * 2)

def apply_kernel(field_in, weights):
    padded = jnp.pad(field_in, ((2, 2), (0, 0), (0, 0), (1, 1)))
    running = jnp.zeros(field_in.shape, jnp.float32)
    for tap_x in range(KX):
        for tap_z in range(KZ):
            window = padded[tap_x:tap_x + NX, :, :, tap_z:tap_z + NZ]
            running = running + jnp.einsum('oi,xyiz->xyoz', weights[tap_x, tap_z], window, precision=lax.Precision.HIGHEST)
    return running

def apply_adjoint(field_in, weights):
    padded = jnp.pad(field_in, ((2, 2), (0, 0), (0, 0), (1, 1)))
    running = jnp.zeros(field_in.shape, jnp.float32)
    for tap_x in range(KX):
        for tap_z in range(KZ):
            window = padded[4 - tap_x:4 - tap_x + NX, :, :, 2 - tap_z:2 - tap_z + NZ]
            running = running + jnp.einsum('oi,xyoz->xyiz', weights[tap_x, tap_z], window, precision=lax.Precision.HIGHEST)
    return running

def second_difference(field_in):
    padded = jnp.pad(field_in, ((1, 1), (0, 0), (0, 0), (0, 0), (0, 0)))
    return padded[:-2] - 2.0 * padded[1:-1] + padded[2:]

def reference(kspace_grid, samples, interp_matrix, kernel_real, kernel_imag, segment_line, segment_readout, segment_count):
    weights = real_form(kernel_real, kernel_imag)
    rounded = kspace_grid.astype(jnp.bfloat16)
    grid_wide = lax.optimization_barrier(rounded).astype(jnp.float32)
    conv_out = lax.map(lambda plane_set: apply_kernel(plane_set, weights), grid_wide)
    spirit = conv_out - kspace_grid
    spirit_wide = lax.optimization_barrier(spirit.astype(jnp.bfloat16)).astype(jnp.float32)
    adjoint = lax.map(lambda plane_set: apply_adjoint(plane_set, weights), spirit_wide)
    lines_all = grid_wide.reshape(PHASES, TILE_COUNT, LINES, CH, NZ)
    interp_wide = interp_matrix.astype(jnp.float32)
    slot_live = (jnp.arange(CAP)[None, None, None, :] < segment_count[..., None]).astype(jnp.float32)

    def phase_readings(phase_item):
        lines_phase, interp_phase, line_phase, read_phase, live_phase = phase_item

        def source_step(running, source_item):
            lines_tile, interp_tile, line_tile, read_tile, live_tile = source_item
            gathered = lines_tile[line_tile]
            partial_value = jnp.einsum('ocqz,sz->ocqs', gathered, interp_tile, precision=lax.Precision.HIGHEST)
            partial_value = partial_value * live_tile[:, :, None, None]
            readout_pick = (read_tile[:, :, None] == jnp.arange(READ_DEV)[None, None, :]).astype(jnp.float32)
            running = running + jnp.einsum('ocr,ocqs->orqs', readout_pick, partial_value, precision=lax.Precision.HIGHEST)
            return (running, None)
        start = jnp.zeros((TILE_COUNT, READ_DEV, CH, SEG), jnp.float32)
        running, unused = lax.scan(source_step, start, (lines_phase, interp_phase, line_phase, read_phase, live_phase))
        return running
    readings = lax.map(phase_readings, (lines_all, interp_wide, segment_line, segment_readout, slot_live))
    data_residual = readings.reshape(PHASES, READS, COILS, 2 * SEG) - samples
    residual_wide = lax.optimization_barrier(data_residual.astype(jnp.bfloat16)).astype(jnp.float32)
    residual_blocks = residual_wide.reshape(PHASES, TILE_COUNT, READ_DEV, CH, SEG)

    def phase_grad(phase_item):
        residual_phase, interp_phase, line_phase, read_phase, live_phase = phase_item

        def source_step(unused_carry, source_item):
            interp_tile, line_tile, read_tile, live_tile = source_item
            readout_pick = (read_tile[:, :, None] == jnp.arange(READ_DEV)[None, None, :]).astype(jnp.float32)
            slot_rows = jnp.einsum('ocr,orqs->ocqs', readout_pick, residual_phase, precision=lax.Precision.HIGHEST)
            spread = jnp.einsum('ocqs,sz->ocqz', slot_rows, interp_tile, precision=lax.Precision.HIGHEST)
            line_place = (line_tile[:, :, None] == jnp.arange(LINES)[None, None, :]).astype(jnp.float32) * live_tile[:, :, None]
            return (unused_carry, jnp.einsum('ocl,ocqz->lqz', line_place, spread, precision=lax.Precision.HIGHEST))
        unused, line_grads = lax.scan(source_step, jnp.zeros((), jnp.float32), (interp_phase, line_phase, read_phase, live_phase))
        return line_grads
    data_grad = lax.map(phase_grad, (residual_blocks, interp_wide, segment_line, segment_readout, slot_live))
    data_grad = data_grad.reshape(PHASES, NX, NY, CH, NZ)
    phase_bend = second_difference(second_difference(kspace_grid))
    gradient = data_grad + SPIRIT_WEIGHT * (adjoint - spirit) + PHASE_WEIGHT * phase_bend
    return (gradient, data_residual)
```

```python
import functools

import jax
import jax.numpy as jnp
from jax import lax
from jax.experimental import pallas as pl
from jax.experimental.pallas import tpu as pltpu
from jax.sharding import PartitionSpec as P

SPIRIT_WEIGHT = 1.0
PHASE_WEIGHT = 0.15

BF = jnp.bfloat16
F32 = jnp.float32


def dot(a, b):
    return jnp.dot(a, b, preferred_element_type=F32)


def dot_t(a, b):
    return lax.dot_general(a, b, (((1,), (1,)), ((), ())), preferred_element_type=F32)


def onehot(mask):
    return jnp.where(mask, 1.0, 0.0).astype(BF)


def iota(shape, dim):
    return lax.broadcasted_iota(jnp.int32, shape, dim)


def build_matrix(taps_ref, out_ref, coils, kx, kz, planes, adjoint):
    taps = taps_ref[...]
    half = kx * coils
    chan = 2 * coils
    width = (planes + kx - 1) * chan
    src = iota((half, width), 0)
    col = iota((half, width), 1)
    rows = iota((chan, chan), 0)
    cols = iota((chan, chan), 1)
    weave = onehot(rows == jnp.where(cols < coils, 2 * cols, 2 * (cols - coils) + 1))
    tap_a = src // coils
    coil = src % coils
    for x in range(planes):
        plane = (x + kx - 1 - tap_a) if adjoint else (x + tap_a)
        base = plane * chan + 2 * coil
        even = jnp.where(col == base, 1.0, 0.0)
        odd = jnp.where(col == base + 1, 1.0, 0.0)
        sign = -1.0 if not adjoint else 1.0
        first = jnp.concatenate([even, sign * odd], axis=0).astype(BF)
        second = jnp.concatenate([odd, -sign * even], axis=0).astype(BF)
        upper = dot(taps, first).astype(BF)
        lower = dot(taps, second).astype(BF)
        for c in range(kz):
            both = jnp.concatenate(
                [upper[c * coils : (c + 1) * coils], lower[c * coils : (c + 1) * coils]], axis=0
            )
            row = (c * planes + x) * chan
            out_ref[row : row + chan, :] = dot(weave, both).astype(BF)


def stencil(weights, window, rows, up):
    prod = dot(weights, window)
    depth = prod.shape[1]
    lane = iota((rows, depth), 1)
    first, mid, last = prod[:rows], prod[rows : 2 * rows], prod[2 * rows : 3 * rows]
    if up:
        first, last = last, first
    first = jnp.where(lane == 0, 0.0, pltpu.roll(first, 1, 1))
    last = jnp.where(lane == depth - 1, 0.0, pltpu.roll(last, depth - 1, 1))
    return first + mid + last


def kernel(
    dims,
    meta,
    grid,
    samples,
    interp,
    fwd_taps,
    adj_taps,
    grad,
    resid,
    ext,
    ext2,
    plo,
    phi,
    image,
    snd,
    rcv,
    back_snd,
    back_rcv,
    racc,
    lacc,
    w_fwd,
    w_adj,
    halo_send,
    halo_recv,
    ph_send,
    ph_recv,
    a_send,
    a_recv,
    b_send,
    b_recv,
):
    slabs, tiles, phases, planes, rows_y, chan, depth, kx, kz, cap, reads = dims
    coils = chan // 2
    lines = planes * rows_y
    own = planes * chan
    slots = phases * cap
    seg = interp.shape[2]
    slab = lax.axis_index("phases")
    me = lax.axis_index("tiles")

    barrier = pltpu.get_barrier_semaphore()

    @pl.loop(1, tiles)
    def _(k):
        pl.semaphore_signal(barrier, inc=1, device_id={"tiles": lax.rem(me + k, tiles)})

    @pl.when(slab > 0)
    def _():
        pl.semaphore_signal(barrier, inc=1, device_id={"phases": slab - 1})

    @pl.when(slab < slabs - 1)
    def _():
        pl.semaphore_signal(barrier, inc=1, device_id={"phases": slab + 1})

    for p in range(phases):
        for x in range(planes):
            for y in range(rows_y):
                ext[p, y, own + x * chan : own + (x + 1) * chan, :] = grid[p, x, y].astype(BF)

    def zero_edges(ref):
        @pl.when(me == 0)
        def _():
            ref[:, :, :own, :] = jnp.zeros((phases, rows_y, own, depth), BF)

        @pl.when(me == tiles - 1)
        def _():
            ref[:, :, 2 * own :, :] = jnp.zeros((phases, rows_y, own, depth), BF)

    zero_edges(ext)
    zero_edges(ext2)

    @pl.when(slab == 0)
    def _():
        plo[...] = jnp.zeros(plo.shape, BF)

    @pl.when(slab == slabs - 1)
    def _():
        phi[...] = jnp.zeros(phi.shape, BF)

    rows_i = iota((chan, chan), 0)
    cols_i = iota((chan, chan), 1)
    split = onehot(cols_i == jnp.where(rows_i < coils, 2 * rows_i, 2 * (rows_i - coils) + 1))
    weave = onehot(rows_i == jnp.where(cols_i < coils, 2 * cols_i, 2 * (cols_i - coils) + 1))
    zero_w = jnp.zeros((seg, depth), BF)
    for p in range(phases):
        w = interp[p, 0]
        w_even = jnp.concatenate([w, zero_w], axis=0)
        w_odd = jnp.concatenate([zero_w, w], axis=0)
        for l in range(lines):
            x, y = l // rows_y, l % rows_y
            parted = dot(split, ext[p, y, own + x * chan : own + (x + 1) * chan, :]).astype(BF)
            image[p * lines + l] = dot_t(parted[:coils], w_even) + dot_t(parted[coils:], w_odd)

    peers = tiles - 1 + jnp.where(slab > 0, 1, 0) + jnp.where(slab < slabs - 1, 1, 0)
    pl.semaphore_wait(barrier, peers)

    def halo(ref, index, right):
        if right:
            src, dst, target = (own, 2 * own), (0, own), me + 1
        else:
            src, dst, target = (own, 2 * own), (2 * own, 3 * own), me - 1
        return pltpu.make_async_remote_copy(
            src_ref=ref.at[:, :, src[0] : src[1], :],
            dst_ref=ref.at[:, :, dst[0] : dst[1], :],
            send_sem=halo_send.at[index],
            recv_sem=halo_recv.at[index],
            device_id={"tiles": target},
        )

    def start_halo(ref, index):
        @pl.when(me < tiles - 1)
        def _():
            halo(ref, index, True).start()

        @pl.when(me > 0)
        def _():
            halo(ref, index + 1, False).start()

    def wait_halo(ref, index):
        @pl.when(me > 0)
        def _():
            halo(ref, index, True).wait_recv()

        @pl.when(me < tiles - 1)
        def _():
            halo(ref, index + 1, False).wait_recv()

    def end_halo(ref, index):
        @pl.when(me < tiles - 1)
        def _():
            halo(ref, index, True).wait_send()

        @pl.when(me > 0)
        def _():
            halo(ref, index + 1, False).wait_send()

    def phase_copy(up):
        return pltpu.make_async_remote_copy(
            src_ref=ext.at[:, :, own : 2 * own, :],
            dst_ref=plo if up else phi,
            send_sem=ph_send.at[0 if up else 1],
            recv_sem=ph_recv.at[0 if up else 1],
            device_id={"phases": slab + 1 if up else slab - 1},
        )

    start_halo(ext, 0)

    def line_of(p, o, c):
        return meta[p, o * cap + c]

    def read_of(p, o, c):
        return meta[p, (tiles + o) * cap + c]

    def live_of(p, o, c):
        return jnp.where(c < meta[p, 2 * tiles * cap + o], 1.0, 0.0)

    pad = snd.shape[1] - slots * coils

    def fill(o, ref):
        ids = jnp.zeros((pad, 2 * seg), F32)
        row = iota((pad, 2 * seg), 0)
        for p in range(phases):
            for c in range(cap):
                s = p * cap + c
                value = image[p * lines + line_of(p, o, c)] * live_of(p, o, c)
                ref[o, s * coils : (s + 1) * coils, :] = value.astype(BF)
                ids = jnp.where(row == s, read_of(p, o, c).astype(F32), ids)
        ref[o, slots * coils :, :] = ids.astype(BF)

    def there(o):
        return pltpu.make_async_remote_copy(
            src_ref=snd.at[o],
            dst_ref=rcv.at[me],
            send_sem=a_send.at[o],
            recv_sem=a_recv.at[me],
            device_id={"tiles": o},
        )

    def arrived(t):
        return pltpu.make_async_remote_copy(
            src_ref=snd.at[t],
            dst_ref=rcv.at[t],
            send_sem=a_send.at[t],
            recv_sem=a_recv.at[t],
            device_id={"tiles": t},
        )

    def back(t):
        return pltpu.make_async_remote_copy(
            src_ref=back_snd.at[t],
            dst_ref=back_rcv.at[me],
            send_sem=b_send.at[t],
            recv_sem=b_recv.at[me],
            device_id={"tiles": t},
        )

    def returned(o):
        return pltpu.make_async_remote_copy(
            src_ref=back_snd.at[o],
            dst_ref=back_rcv.at[o],
            send_sem=b_send.at[o],
            recv_sem=b_recv.at[o],
            device_id={"tiles": o},
        )

    @pl.loop(1, tiles)
    def _(k):
        o = lax.rem(me + k, tiles)
        fill(o, snd)
        there(o).start()

    fill(me, rcv)

    @pl.when(slab < slabs - 1)
    def _():
        phase_copy(True).start()

    @pl.when(slab > 0)
    def _():
        phase_copy(False).start()

    build_matrix(fwd_taps, w_fwd, coils, kx, kz, planes, False)
    build_matrix(adj_taps, w_adj, coils, kx, kz, planes, True)

    wait_halo(ext, 0)
    for p in range(phases):
        for y in range(rows_y):
            out = stencil(w_fwd[...], ext[p, y], own, False)
            for x in range(planes):
                rest = out[x * chan : (x + 1) * chan] - grid[p, x, y]
                grad[p, x, y] = -SPIRIT_WEIGHT * rest
                ext2[p, y, own + x * chan : own + (x + 1) * chan, :] = rest.astype(BF)
    start_halo(ext2, 2)

    for p in range(phases):
        for r in range(reads):
            racc[p, r] = -samples[p, r]

    def add_from(t):
        ids = rcv[t, slots * coils :, :].astype(F32)
        for p in range(phases):
            for c in range(cap):
                s = p * cap + c
                value = rcv[t, s * coils : (s + 1) * coils, :].astype(F32)
                own_id = jnp.broadcast_to(ids[s : s + 1], value.shape)
                for r in range(reads):
                    racc[p, r] = racc[p, r] + jnp.where(own_id == r, value, 0.0)

    add_from(me)

    @pl.loop(1, tiles)
    def _(k):
        t = lax.rem(me + tiles - k, tiles)
        arrived(t).wait_recv()
        add_from(t)

    for p in range(phases):
        for r in range(reads):
            value = racc[p, r]
            resid[p, r] = value
            racc[p, r] = value.astype(BF).astype(F32)

    def pick_for(t, ref):
        ids = rcv[t, slots * coils :, :].astype(F32)
        for p in range(phases):
            for c in range(cap):
                s = p * cap + c
                own_id = jnp.broadcast_to(ids[s : s + 1], (coils, 2 * seg))
                value = jnp.zeros((coils, 2 * seg), F32)
                for r in range(reads):
                    value = jnp.where(own_id == r, racc[p, r], value)
                ref[t, s * coils : (s + 1) * coils, :] = value.astype(BF)

    @pl.loop(1, tiles)
    def _(k):
        t = lax.rem(me + k, tiles)
        pick_for(t, back_snd)
        back(t).start()

    pick_for(me, back_rcv)

    @pl.when(slab > 0)
    def _():
        phase_copy(True).wait_recv()

    @pl.when(slab < slabs - 1)
    def _():
        phase_copy(False).wait_recv()

    below = jnp.where(slab > 0, 1.0, 0.0)
    above = jnp.where(slab < slabs - 1, 1.0, 0.0)
    for y in range(rows_y):
        for x in range(planes):
            part = slice(x * chan, (x + 1) * chan)
            field = [plo[phases - 2, y, part, :].astype(F32), plo[phases - 1, y, part, :].astype(F32)]
            field += [grid[p, x, y] for p in range(phases)]
            field += [phi[0, y, part, :].astype(F32), phi[1, y, part, :].astype(F32)]
            diff = [field[i] - 2.0 * field[i + 1] + field[i + 2] for i in range(phases + 2)]
            diff[0] = diff[0] * below
            diff[-1] = diff[-1] * above
            for p in range(phases):
                bend = diff[p] - 2.0 * diff[p + 1] + diff[p + 2]
                grad[p, x, y] = grad[p, x, y] + PHASE_WEIGHT * bend

    wait_halo(ext2, 2)
    for p in range(phases):
        for y in range(rows_y):
            out = stencil(w_adj[...], ext2[p, y], own, True)
            for x in range(planes):
                part = out[x * chan : (x + 1) * chan]
                grad[p, x, y] = grad[p, x, y] + SPIRIT_WEIGHT * part

    for i in range(phases * lines):
        lacc[i] = jnp.zeros((coils, 2 * seg), F32)

    def spread_from(o):
        for p in range(phases):
            for c in range(cap):
                s = p * cap + c
                value = back_rcv[o, s * coils : (s + 1) * coils, :].astype(F32) * live_of(p, o, c)
                line = line_of(p, o, c)
                for l in range(lines):
                    weight = jnp.where(line == l, 1.0, 0.0)
                    lacc[p * lines + l] = lacc[p * lines + l] + value * weight

    spread_from(me)

    @pl.loop(1, tiles)
    def _(k):
        o = lax.rem(me + tiles - k, tiles)
        returned(o).wait_recv()
        spread_from(o)

    lane = iota((coils, 2 * seg), 1)
    for p in range(phases):
        w = interp[p, 0]
        four = jnp.concatenate([w, w, w, w], axis=0)
        for l in range(lines):
            x, y = l // rows_y, l % rows_y
            total = lacc[p * lines + l]
            high = total.astype(BF).astype(F32)
            rest = total - high
            even = [jnp.where(lane < seg, v, 0.0) for v in (high, rest)]
            odd = [jnp.where(lane < seg, 0.0, v) for v in (high, rest)]
            both = jnp.concatenate(
                [jnp.concatenate(even, axis=1), jnp.concatenate(odd, axis=1)], axis=0
            ).astype(BF)
            woven = dot(weave, both).astype(BF)
            grad[p, x, y] = grad[p, x, y] + dot(woven, four)

    end_halo(ext, 0)
    end_halo(ext2, 2)

    @pl.when(slab < slabs - 1)
    def _():
        phase_copy(True).wait_send()

    @pl.when(slab > 0)
    def _():
        phase_copy(False).wait_send()

    @pl.loop(1, tiles)
    def _(k):
        o = lax.rem(me + k, tiles)
        there(o).wait_send()
        back(o).wait_send()


def on_device(
    slabs,
    tiles,
    kspace_grid,
    samples,
    interp_matrix,
    kernel_real,
    kernel_imag,
    segment_line,
    segment_readout,
    segment_count,
):
    phases, planes, rows_y, chan, depth = kspace_grid.shape
    kx, kz, coils, _ = kernel_real.shape
    cap = segment_line.shape[3]
    reads = samples.shape[1]
    seg = interp_matrix.shape[2]
    own = planes * chan
    slots = phases * cap
    message = slots * coils + 16 * -(-slots // 16)
    lines = planes * rows_y
    width = (planes + kx - 1) * chan
    meta = jnp.concatenate(
        [
            segment_line.reshape(phases, -1),
            segment_readout.reshape(phases, -1),
            segment_count.reshape(phases, -1),
        ],
        axis=1,
    )
    both = jnp.stack([kernel_real, kernel_imag])
    fwd_taps = jnp.transpose(both, (2, 3, 0, 1, 4)).reshape(kz * coils, 2 * kx * coils)
    adj_taps = jnp.transpose(both, (2, 4, 0, 1, 3)).reshape(kz * coils, 2 * kx * coils)
    dims = (slabs, tiles, phases, planes, rows_y, chan, depth, kx, kz, cap, reads)
    vmem = pl.BlockSpec(memory_space=pltpu.VMEM)
    dma = pltpu.SemaphoreType.DMA
    return pl.pallas_call(
        functools.partial(kernel, dims),
        out_shape=(
            jax.ShapeDtypeStruct(kspace_grid.shape, F32),
            jax.ShapeDtypeStruct(samples.shape, F32),
        ),
        in_specs=[pl.BlockSpec(memory_space=pltpu.SMEM)] + [vmem] * 5,
        out_specs=(vmem, vmem),
        scratch_shapes=[
            pltpu.VMEM((phases, rows_y, 3 * own, depth), BF),
            pltpu.VMEM((phases, rows_y, 3 * own, depth), BF),
            pltpu.VMEM((phases, rows_y, own, depth), BF),
            pltpu.VMEM((phases, rows_y, own, depth), BF),
            pltpu.VMEM((phases * lines, coils, 2 * seg), F32),
            pltpu.VMEM((tiles, message, 2 * seg), BF),
            pltpu.VMEM((tiles, message, 2 * seg), BF),
            pltpu.VMEM((tiles, slots * coils, 2 * seg), BF),
            pltpu.VMEM((tiles, slots * coils, 2 * seg), BF),
            pltpu.VMEM((phases, reads, coils, 2 * seg), F32),
            pltpu.VMEM((phases * lines, coils, 2 * seg), F32),
            pltpu.VMEM((kz * own, width), BF),
            pltpu.VMEM((kz * own, width), BF),
            dma((4,)),
            dma((4,)),
            dma((2,)),
            dma((2,)),
            dma((tiles,)),
            dma((tiles,)),
            dma((tiles,)),
            dma((tiles,)),
        ],
        compiler_params=pltpu.CompilerParams(
            collective_id=0, has_side_effects=True, vmem_limit_bytes=48 * 1024 * 1024
        ),
    )(meta, kspace_grid, samples, interp_matrix, fwd_taps, adj_taps)


def solution(mesh):
    return jax.shard_map(
        functools.partial(on_device, mesh.shape["phases"], mesh.shape["tiles"]),
        mesh=mesh,
        in_specs=(
            P("phases", "tiles", None, None, None),
            P("phases", "tiles", None, None),
            P("phases", "tiles", None, None),
            P(),
            P(),
            P("phases", "tiles", None, None),
            P("phases", "tiles", None, None),
            P("phases", "tiles", None),
        ),
        out_specs=(P("phases", "tiles", None, None, None), P("phases", "tiles", None, None)),
        check_vma=False,
    )
```

```python
import functools

import jax
import jax.numpy as jnp
from jax import lax
from jax.experimental import pallas as pl
from jax.experimental.pallas import tpu as pltpu
from jax.sharding import PartitionSpec as P

SPIRIT_WEIGHT = 1.0
PHASE_WEIGHT = 0.15

BF = jnp.bfloat16
F32 = jnp.float32


def dot(a, b):
    return jnp.dot(a, b, preferred_element_type=F32)


def dot_t(a, b):
    return lax.dot_general(a, b, (((1,), (1,)), ((), ())), preferred_element_type=F32)


def onehot(mask):
    return jnp.where(mask, 1.0, 0.0).astype(BF)


def iota(shape, dim):
    return lax.broadcasted_iota(jnp.int32, shape, dim)


def build_matrices(real_ref, imag_ref, fwd_ref, adj_ref, planes):
    kx, kz, coils, _ = real_ref.shape
    chan = 2 * coils
    real = real_ref[...].reshape(kx * kz * coils, coils)
    imag = imag_ref[...].reshape(kx * kz * coils, coils)
    src = iota((coils, 2 * chan), 0)
    col = iota((coils, 2 * chan), 1)
    rows = iota((chan, chan), 0)
    cols = iota((chan, chan), 1)
    weave = onehot(rows == jnp.where(cols < coils, 2 * cols, 2 * (cols - coils) + 1))
    unit = onehot(iota((chan, 2 * chan), 0) == iota((chan, 2 * chan), 1))
    sides = []
    for side in range(2):
        even = onehot(col == side * chan + 2 * src)
        odd = onehot(col == side * chan + 2 * src + 1)
        upper = (dot(real, even) - dot(imag, odd)).astype(BF)
        lower = (dot(real, odd) + dot(imag, even)).astype(BF)
        blocks = {}
        for a in range(kx):
            for c in range(kz):
                at = slice((a * kz + c) * coils, (a * kz + c + 1) * coils)
                both = jnp.concatenate([upper[at], lower[at]], axis=0)
                blocks[a, c] = dot(weave, both)
        sides.append(blocks)
    zero = jnp.zeros((chan, 2 * chan), F32)
    for c in range(kz):
        for x in range(planes):
            row = (c * planes + x) * chan
            for q in range((planes + kx - 1) // 2):
                at = slice(2 * q * chan, 2 * (q + 1) * chan)
                left, right = 2 * q - x, 2 * q + 1 - x
                value = sides[0].get((left, c), zero) + sides[1].get((right, c), zero)
                fwd_ref[row : row + chan, at] = value.astype(BF)
                left, right = x + kx - 1 - 2 * q, x + kx - 2 - 2 * q
                pair = jnp.concatenate(
                    [sides[0].get((left, c), zero), sides[0].get((right, c), zero)], axis=0
                )
                adj_ref[row : row + chan, at] = dot_t(unit, pair.astype(BF)).astype(BF)


def stencil(weights, window, rows, up):
    prod = dot(weights, window)
    depth = prod.shape[1]
    lane = iota((rows, depth), 1)
    first, mid, last = prod[:rows], prod[rows : 2 * rows], prod[2 * rows : 3 * rows]
    if up:
        first, last = last, first
    first = jnp.where(lane == 0, 0.0, pltpu.roll(first, 1, 1))
    last = jnp.where(lane == depth - 1, 0.0, pltpu.roll(last, depth - 1, 1))
    return first + mid + last


def kernel(
    dims,
    line_ids,
    read_ids,
    counts,
    grid_in,
    samples_in,
    interp_in,
    real_in,
    imag_in,
    grad,
    resid,
    ext,
    ext2,
    plo,
    phi,
    image,
    snd,
    rcv,
    back_snd,
    back_rcv,
    racc,
    lacc,
    w_fwd,
    w_adj,
    halo_send,
    halo_recv,
    ph_send,
    ph_recv,
    a_send,
    a_recv,
    b_send,
    b_recv,
    grid,
    samples,
    interp,
    taps_real,
    taps_imag,
    in_sem,
):
    slabs, tiles, phases, planes, rows_y, chan, depth, kx, kz, cap, reads = dims
    coils = chan // 2
    lines = planes * rows_y
    own = planes * chan
    slots = phases * cap
    seg = interp_in.shape[2]
    loads = [
        pltpu.make_async_copy(src, dst, in_sem.at[i])
        for i, (src, dst) in enumerate(
            (
                (grid_in, grid),
                (interp_in, interp),
                (real_in, taps_real),
                (imag_in, taps_imag),
                (samples_in, samples),
            )
        )
    ]
    for load in loads:
        load.start()
    slab = lax.axis_index("phases")
    me = lax.axis_index("tiles")

    barrier = pltpu.get_barrier_semaphore()

    @pl.loop(1, tiles)
    def _(k):
        pl.semaphore_signal(barrier, inc=1, device_id={"tiles": lax.rem(me + k, tiles)})

    @pl.when(slab > 0)
    def _():
        pl.semaphore_signal(barrier, inc=1, device_id={"phases": slab - 1})

    @pl.when(slab < slabs - 1)
    def _():
        pl.semaphore_signal(barrier, inc=1, device_id={"phases": slab + 1})

    loads[0].wait()
    for p in range(phases):
        for x in range(planes):
            for y in range(rows_y):
                ext[p, y, own + x * chan : own + (x + 1) * chan, :] = grid[p, x, y].astype(BF)

    def zero_edges(ref):
        @pl.when(me == 0)
        def _():
            ref[:, :, :own, :] = jnp.zeros((phases, rows_y, own, depth), BF)

        @pl.when(me == tiles - 1)
        def _():
            ref[:, :, 2 * own :, :] = jnp.zeros((phases, rows_y, own, depth), BF)

    zero_edges(ext)
    zero_edges(ext2)

    @pl.when(slab == 0)
    def _():
        plo[...] = jnp.zeros(plo.shape, BF)

    @pl.when(slab == slabs - 1)
    def _():
        phi[...] = jnp.zeros(phi.shape, BF)

    for load in loads[1:]:
        load.wait()

    rows_i = iota((chan, chan), 0)
    cols_i = iota((chan, chan), 1)
    split = onehot(cols_i == jnp.where(rows_i < coils, 2 * rows_i, 2 * (rows_i - coils) + 1))
    weave = onehot(rows_i == jnp.where(cols_i < coils, 2 * cols_i, 2 * (cols_i - coils) + 1))
    zero_w = jnp.zeros((seg, depth), BF)
    for p in range(phases):
        w = interp[p, 0]
        w_even = jnp.concatenate([w, zero_w], axis=0)
        w_odd = jnp.concatenate([zero_w, w], axis=0)
        for l in range(lines):
            x, y = l // rows_y, l % rows_y
            parted = dot(split, ext[p, y, own + x * chan : own + (x + 1) * chan, :]).astype(BF)
            image[p * lines + l] = dot_t(parted[:coils], w_even) + dot_t(parted[coils:], w_odd)

    peers = tiles - 1 + jnp.where(slab > 0, 1, 0) + jnp.where(slab < slabs - 1, 1, 0)
    pl.semaphore_wait(barrier, peers)

    def halo(ref, index, right, p):
        if right:
            src, dst, target = (own, 2 * own), (0, own), me + 1
        else:
            src, dst, target = (own, 2 * own), (2 * own, 3 * own), me - 1
        return pltpu.make_async_remote_copy(
            src_ref=ref.at[p, :, src[0] : src[1], :],
            dst_ref=ref.at[p, :, dst[0] : dst[1], :],
            send_sem=halo_send.at[index],
            recv_sem=halo_recv.at[index],
            device_id={"tiles": target},
        )

    def start_halo(ref, index, p):
        @pl.when(me < tiles - 1)
        def _():
            halo(ref, index + 2 * p, True, p).start()

        @pl.when(me > 0)
        def _():
            halo(ref, index + 2 * p + 1, False, p).start()

    def wait_halo(ref, index, p):
        @pl.when(me > 0)
        def _():
            halo(ref, index + 2 * p, True, p).wait_recv()

        @pl.when(me < tiles - 1)
        def _():
            halo(ref, index + 2 * p + 1, False, p).wait_recv()

    def end_halo(ref, index, p):
        @pl.when(me < tiles - 1)
        def _():
            halo(ref, index + 2 * p, True, p).wait_send()

        @pl.when(me > 0)
        def _():
            halo(ref, index + 2 * p + 1, False, p).wait_send()

    def phase_copy(up):
        return pltpu.make_async_remote_copy(
            src_ref=ext.at[:, :, own : 2 * own, :],
            dst_ref=plo if up else phi,
            send_sem=ph_send.at[0 if up else 1],
            recv_sem=ph_recv.at[0 if up else 1],
            device_id={"phases": slab + 1 if up else slab - 1},
        )

    @pl.when(slab < slabs - 1)
    def _():
        phase_copy(True).start()

    @pl.when(slab > 0)
    def _():
        phase_copy(False).start()

    for p in range(phases):
        start_halo(ext, 0, p)

    def line_of(p, o, c):
        return line_ids[p, 0, c, o]

    def read_of(p, o, c):
        return read_ids[p, 0, c, o]

    def live_of(p, o, c):
        return jnp.where(c < counts[p, 0, o], 1.0, 0.0)

    pad = snd.shape[1] - slots * coils

    def fill(o, ref):
        ids = jnp.zeros((pad, 2 * seg), F32)
        row = iota((pad, 2 * seg), 0)
        for p in range(phases):
            for c in range(cap):
                s = p * cap + c
                value = image[p * lines + line_of(p, o, c)] * live_of(p, o, c)
                ref[o, s * coils : (s + 1) * coils, :] = value.astype(BF)
                ids = jnp.where(row == s, read_of(p, o, c).astype(F32), ids)
        ref[o, slots * coils :, :] = ids.astype(BF)

    def there(o):
        return pltpu.make_async_remote_copy(
            src_ref=snd.at[o],
            dst_ref=rcv.at[me],
            send_sem=a_send.at[o],
            recv_sem=a_recv.at[me],
            device_id={"tiles": o},
        )

    def arrived(t):
        return pltpu.make_async_remote_copy(
            src_ref=snd.at[t],
            dst_ref=rcv.at[t],
            send_sem=a_send.at[t],
            recv_sem=a_recv.at[t],
            device_id={"tiles": t},
        )

    def back(t):
        return pltpu.make_async_remote_copy(
            src_ref=back_snd.at[t],
            dst_ref=back_rcv.at[me],
            send_sem=b_send.at[t],
            recv_sem=b_recv.at[me],
            device_id={"tiles": t},
        )

    def returned(o):
        return pltpu.make_async_remote_copy(
            src_ref=back_snd.at[o],
            dst_ref=back_rcv.at[o],
            send_sem=b_send.at[o],
            recv_sem=b_recv.at[o],
            device_id={"tiles": o},
        )

    @pl.loop(1, tiles)
    def _(k):
        o = lax.rem(me + k, tiles)
        fill(o, snd)
        there(o).start()

    fill(me, rcv)

    build_matrices(taps_real, taps_imag, w_fwd, w_adj, planes)

    for p in range(phases):
        wait_halo(ext, 0, p)
        for y in range(rows_y):
            out = stencil(w_fwd[...], ext[p, y], own, False)
            for x in range(planes):
                rest = out[x * chan : (x + 1) * chan] - grid[p, x, y]
                grad[p, x, y] = -SPIRIT_WEIGHT * rest
                ext2[p, y, own + x * chan : own + (x + 1) * chan, :] = rest.astype(BF)
        start_halo(ext2, 2 * phases, p)

    for p in range(phases):
        for r in range(reads):
            racc[p, r] = -samples[p, r]

    def add_from(t):
        ids = rcv[t, slots * coils :, :].astype(F32)
        for p in range(phases):
            for c in range(cap):
                s = p * cap + c
                value = rcv[t, s * coils : (s + 1) * coils, :].astype(F32)
                own_id = jnp.broadcast_to(ids[s : s + 1], value.shape)
                for r in range(reads):
                    racc[p, r] = racc[p, r] + jnp.where(own_id == r, value, 0.0)

    add_from(me)

    @pl.loop(1, tiles)
    def _(k):
        t = lax.rem(me + tiles - k, tiles)
        arrived(t).wait_recv()
        add_from(t)

    for p in range(phases):
        for r in range(reads):
            value = racc[p, r]
            resid[p, r] = value
            racc[p, r] = value.astype(BF).astype(F32)

    def pick_for(t, ref):
        ids = rcv[t, slots * coils :, :].astype(F32)
        for p in range(phases):
            for c in range(cap):
                s = p * cap + c
                own_id = jnp.broadcast_to(ids[s : s + 1], (coils, 2 * seg))
                value = jnp.zeros((coils, 2 * seg), F32)
                for r in range(reads):
                    value = jnp.where(own_id == r, racc[p, r], value)
                ref[t, s * coils : (s + 1) * coils, :] = value.astype(BF)

    @pl.loop(1, tiles)
    def _(k):
        t = lax.rem(me + k, tiles)
        pick_for(t, back_snd)
        back(t).start()

    pick_for(me, back_rcv)

    @pl.when(slab > 0)
    def _():
        phase_copy(True).wait_recv()

    @pl.when(slab < slabs - 1)
    def _():
        phase_copy(False).wait_recv()

    below = jnp.where(slab > 0, 1.0, 0.0)
    above = jnp.where(slab < slabs - 1, 1.0, 0.0)
    for y in range(rows_y):
        for x in range(planes):
            part = slice(x * chan, (x + 1) * chan)
            field = [plo[phases - 2, y, part, :].astype(F32), plo[phases - 1, y, part, :].astype(F32)]
            field += [grid[p, x, y] for p in range(phases)]
            field += [phi[0, y, part, :].astype(F32), phi[1, y, part, :].astype(F32)]
            diff = [field[i] - 2.0 * field[i + 1] + field[i + 2] for i in range(phases + 2)]
            diff[0] = diff[0] * below
            diff[-1] = diff[-1] * above
            for p in range(phases):
                bend = diff[p] - 2.0 * diff[p + 1] + diff[p + 2]
                grad[p, x, y] = grad[p, x, y] + PHASE_WEIGHT * bend

    for p in range(phases):
        wait_halo(ext2, 2 * phases, p)
        for y in range(rows_y):
            out = stencil(w_adj[...], ext2[p, y], own, True)
            for x in range(planes):
                part = out[x * chan : (x + 1) * chan]
                grad[p, x, y] = grad[p, x, y] + SPIRIT_WEIGHT * part

    for i in range(phases * lines):
        lacc[i] = jnp.zeros((coils, 2 * seg), F32)

    def spread_from(o):
        for p in range(phases):
            for c in range(cap):
                s = p * cap + c
                value = back_rcv[o, s * coils : (s + 1) * coils, :].astype(F32) * live_of(p, o, c)
                line = line_of(p, o, c)
                for l in range(lines):
                    weight = jnp.where(line == l, 1.0, 0.0)
                    lacc[p * lines + l] = lacc[p * lines + l] + value * weight

    spread_from(me)

    @pl.loop(1, tiles)
    def _(k):
        o = lax.rem(me + tiles - k, tiles)
        returned(o).wait_recv()
        spread_from(o)

    lane = iota((coils, 2 * seg), 1)
    for p in range(phases):
        w = interp[p, 0]
        four = jnp.concatenate([w, w, w, w], axis=0)
        for l in range(lines):
            x, y = l // rows_y, l % rows_y
            total = lacc[p * lines + l]
            high = total.astype(BF).astype(F32)
            rest = total - high
            even = [jnp.where(lane < seg, v, 0.0) for v in (high, rest)]
            odd = [jnp.where(lane < seg, 0.0, v) for v in (high, rest)]
            both = jnp.concatenate(
                [jnp.concatenate(even, axis=1), jnp.concatenate(odd, axis=1)], axis=0
            ).astype(BF)
            woven = dot(weave, both).astype(BF)
            grad[p, x, y] = grad[p, x, y] + dot(woven, four)

    for p in range(phases):
        end_halo(ext, 0, p)
        end_halo(ext2, 2 * phases, p)

    @pl.when(slab < slabs - 1)
    def _():
        phase_copy(True).wait_send()

    @pl.when(slab > 0)
    def _():
        phase_copy(False).wait_send()

    @pl.loop(1, tiles)
    def _(k):
        o = lax.rem(me + k, tiles)
        there(o).wait_send()
        back(o).wait_send()


def on_device(
    slabs,
    tiles,
    kspace_grid,
    samples,
    interp_matrix,
    kernel_real,
    kernel_imag,
    segment_line,
    segment_readout,
    segment_count,
):
    phases, planes, rows_y, chan, depth = kspace_grid.shape
    kx, kz, coils, _ = kernel_real.shape
    cap = segment_line.shape[3]
    reads = samples.shape[1]
    seg = interp_matrix.shape[2]
    own = planes * chan
    slots = phases * cap
    message = slots * coils + 16 * -(-slots // 16)
    lines = planes * rows_y
    width = (planes + kx - 1) * chan
    dims = (slabs, tiles, phases, planes, rows_y, chan, depth, kx, kz, cap, reads)
    vmem = pl.BlockSpec(memory_space=pltpu.VMEM)
    dma = pltpu.SemaphoreType.DMA
    return pl.pallas_call(
        functools.partial(kernel, dims),
        out_shape=(
            jax.ShapeDtypeStruct(kspace_grid.shape, F32),
            jax.ShapeDtypeStruct(samples.shape, F32),
        ),
        in_specs=[pl.BlockSpec(memory_space=pltpu.SMEM)] * 3 + [pl.BlockSpec(memory_space=pltpu.HBM)] * 5,
        out_specs=(vmem, vmem),
        scratch_shapes=[
            pltpu.VMEM((phases, rows_y, 3 * own, depth), BF),
            pltpu.VMEM((phases, rows_y, 3 * own, depth), BF),
            pltpu.VMEM((phases, rows_y, own, depth), BF),
            pltpu.VMEM((phases, rows_y, own, depth), BF),
            pltpu.VMEM((phases * lines, coils, 2 * seg), F32),
            pltpu.VMEM((tiles, message, 2 * seg), BF),
            pltpu.VMEM((tiles, message, 2 * seg), BF),
            pltpu.VMEM((tiles, slots * coils, 2 * seg), BF),
            pltpu.VMEM((tiles, slots * coils, 2 * seg), BF),
            pltpu.VMEM((phases, reads, coils, 2 * seg), F32),
            pltpu.VMEM((phases * lines, coils, 2 * seg), F32),
            pltpu.VMEM((kz * own, width), BF),
            pltpu.VMEM((kz * own, width), BF),
            dma((4 * phases,)),
            dma((4 * phases,)),
            dma((2,)),
            dma((2,)),
            dma((tiles,)),
            dma((tiles,)),
            dma((tiles,)),
            dma((tiles,)),
            pltpu.VMEM(kspace_grid.shape, F32),
            pltpu.VMEM(samples.shape, F32),
            pltpu.VMEM(interp_matrix.shape, BF),
            pltpu.VMEM(kernel_real.shape, BF),
            pltpu.VMEM(kernel_imag.shape, BF),
            dma((5,)),
        ],
        compiler_params=pltpu.CompilerParams(
            collective_id=0, has_side_effects=True, vmem_limit_bytes=58 * 1024 * 1024
        ),
    )(
        jnp.transpose(segment_line, (0, 1, 3, 2)),
        jnp.transpose(segment_readout, (0, 1, 3, 2)),
        segment_count,
        kspace_grid,
        samples,
        interp_matrix,
        kernel_real,
        kernel_imag,
    )


def solution(mesh):
    return jax.shard_map(
        functools.partial(on_device, mesh.shape["phases"], mesh.shape["tiles"]),
        mesh=mesh,
        in_specs=(
            P("phases", "tiles", None, None, None),
            P("phases", "tiles", None, None),
            P("phases", "tiles", None, None),
            P(),
            P(),
            P("phases", "tiles", None, None),
            P("phases", "tiles", None, None),
            P("phases", "tiles", None),
        ),
        out_specs=(P("phases", "tiles", None, None, None), P("phases", "tiles", None, None)),
        check_vma=False,
    )
```

```python
import functools

import jax
import jax.numpy as jnp
from jax import lax
from jax.experimental import pallas as pl
from jax.experimental.pallas import tpu as pltpu
from jax.sharding import PartitionSpec as P

SPIRIT_WEIGHT = 1.0
PHASE_WEIGHT = 0.15

BF = jnp.bfloat16
F32 = jnp.float32


def dot(a, b):
    return jnp.dot(a, b, preferred_element_type=F32)


def dot_t(a, b):
    return lax.dot_general(a, b, (((1,), (1,)), ((), ())), preferred_element_type=F32)


def onehot(mask):
    return jnp.where(mask, 1.0, 0.0).astype(BF)


def iota(shape, dim):
    return lax.broadcasted_iota(jnp.int32, shape, dim)


def build_matrices(real_ref, imag_ref, fwd_ref, adj_ref, planes):
    kx, kz, coils, _ = real_ref.shape
    chan = 2 * coils
    real = real_ref[...].reshape(kx * kz * coils, coils)
    imag = imag_ref[...].reshape(kx * kz * coils, coils)
    src = iota((coils, 2 * chan), 0)
    col = iota((coils, 2 * chan), 1)
    rows = iota((chan, chan), 0)
    cols = iota((chan, chan), 1)
    weave = onehot(rows == jnp.where(cols < coils, 2 * cols, 2 * (cols - coils) + 1))
    unit = onehot(iota((chan, 2 * chan), 0) == iota((chan, 2 * chan), 1))
    sides = []
    for side in range(2):
        even = onehot(col == side * chan + 2 * src)
        odd = onehot(col == side * chan + 2 * src + 1)
        upper = (dot(real, even) - dot(imag, odd)).astype(BF)
        lower = (dot(real, odd) + dot(imag, even)).astype(BF)
        blocks = {}
        for a in range(kx):
            for c in range(kz):
                at = slice((a * kz + c) * coils, (a * kz + c + 1) * coils)
                both = jnp.concatenate([upper[at], lower[at]], axis=0)
                blocks[a, c] = dot(weave, both)
        sides.append(blocks)
    zero = jnp.zeros((chan, 2 * chan), F32)
    for c in range(kz):
        for x in range(planes):
            row = (c * planes + x) * chan
            for q in range((planes + kx - 1) // 2):
                at = slice(2 * q * chan, 2 * (q + 1) * chan)
                left, right = 2 * q - x, 2 * q + 1 - x
                value = sides[0].get((left, c), zero) + sides[1].get((right, c), zero)
                fwd_ref[row : row + chan, at] = value.astype(BF)
                left, right = x + kx - 1 - 2 * q, x + kx - 2 - 2 * q
                pair = jnp.concatenate(
                    [sides[0].get((left, c), zero), sides[0].get((right, c), zero)], axis=0
                )
                adj_ref[row : row + chan, at] = dot_t(unit, pair.astype(BF)).astype(BF)


def stencil(weights, window, rows, up):
    prod = dot(weights, window)
    depth = prod.shape[1]
    lane = iota((rows, depth), 1)
    first, mid, last = prod[:rows], prod[rows : 2 * rows], prod[2 * rows : 3 * rows]
    if up:
        first, last = last, first
    first = jnp.where(lane == 0, 0.0, pltpu.roll(first, 1, 1))
    last = jnp.where(lane == depth - 1, 0.0, pltpu.roll(last, depth - 1, 1))
    return first + mid + last


def kernel(
    dims,
    line_ids,
    read_ids,
    counts,
    grid_in,
    samples_in,
    interp_in,
    real_in,
    imag_in,
    grad,
    resid,
    ext,
    ext2,
    plo,
    phi,
    image,
    snd,
    rcv,
    back_snd,
    back_rcv,
    racc,
    lacc,
    w_fwd,
    w_adj,
    halo_send,
    halo_recv,
    ph_send,
    ph_recv,
    a_send,
    a_recv,
    b_send,
    b_recv,
    grid,
    samples,
    interp,
    taps_real,
    taps_imag,
    in_sem,
):
    slabs, tiles, phases, planes, rows_y, chan, depth, kx, kz, cap, reads = dims
    coils = chan // 2
    lines = planes * rows_y
    own = planes * chan
    slots = phases * cap
    seg = interp_in.shape[2]
    loads = [
        pltpu.make_async_copy(src, dst, in_sem.at[i])
        for i, (src, dst) in enumerate(
            (
                (grid_in, grid),
                (interp_in, interp),
                (real_in, taps_real),
                (imag_in, taps_imag),
                (samples_in, samples),
            )
        )
    ]
    for load in loads:
        load.start()
    slab = lax.axis_index("phases")
    me = lax.axis_index("tiles")

    barrier = pltpu.get_barrier_semaphore()

    @pl.loop(1, tiles)
    def _(k):
        pl.semaphore_signal(barrier, inc=1, device_id={"tiles": lax.rem(me + k, tiles)})

    @pl.when(slab > 0)
    def _():
        pl.semaphore_signal(barrier, inc=1, device_id={"phases": slab - 1})

    @pl.when(slab < slabs - 1)
    def _():
        pl.semaphore_signal(barrier, inc=1, device_id={"phases": slab + 1})

    loads[0].wait()
    for p in range(phases):
        for x in range(planes):
            for y in range(rows_y):
                ext[p, y, own + x * chan : own + (x + 1) * chan, :] = grid[p, x, y].astype(BF)

    def zero_edges(ref):
        @pl.when(me == 0)
        def _():
            ref[:, :, :own, :] = jnp.zeros((phases, rows_y, own, depth), BF)

        @pl.when(me == tiles - 1)
        def _():
            ref[:, :, 2 * own :, :] = jnp.zeros((phases, rows_y, own, depth), BF)

    zero_edges(ext)
    zero_edges(ext2)

    @pl.when(slab == 0)
    def _():
        plo[...] = jnp.zeros(plo.shape, BF)

    @pl.when(slab == slabs - 1)
    def _():
        phi[...] = jnp.zeros(phi.shape, BF)

    for load in loads[1:]:
        load.wait()

    rows_i = iota((chan, chan), 0)
    cols_i = iota((chan, chan), 1)
    split = onehot(cols_i == jnp.where(rows_i < coils, 2 * rows_i, 2 * (rows_i - coils) + 1))
    weave = onehot(rows_i == jnp.where(cols_i < coils, 2 * cols_i, 2 * (cols_i - coils) + 1))
    zero_w = jnp.zeros((seg, depth), BF)
    for p in range(phases):
        w = interp[p, 0]
        w_even = jnp.concatenate([w, zero_w], axis=0)
        w_odd = jnp.concatenate([zero_w, w], axis=0)
        for l in range(lines):
            x, y = l // rows_y, l % rows_y
            parted = dot(split, ext[p, y, own + x * chan : own + (x + 1) * chan, :]).astype(BF)
            image[p * lines + l] = dot_t(parted[:coils], w_even) + dot_t(parted[coils:], w_odd)

    peers = tiles - 1 + jnp.where(slab > 0, 1, 0) + jnp.where(slab < slabs - 1, 1, 0)
    pl.semaphore_wait(barrier, peers)

    def halo(ref, index, right, p):
        if right:
            src, dst, target = (own, 2 * own), (0, own), me + 1
        else:
            src, dst, target = (own, 2 * own), (2 * own, 3 * own), me - 1
        return pltpu.make_async_remote_copy(
            src_ref=ref.at[p, :, src[0] : src[1], :],
            dst_ref=ref.at[p, :, dst[0] : dst[1], :],
            send_sem=halo_send.at[index],
            recv_sem=halo_recv.at[index],
            device_id={"tiles": target},
        )

    def start_halo(ref, index, p):
        @pl.when(me < tiles - 1)
        def _():
            halo(ref, index + 2 * p, True, p).start()

        @pl.when(me > 0)
        def _():
            halo(ref, index + 2 * p + 1, False, p).start()

    def wait_halo(ref, index, p):
        @pl.when(me > 0)
        def _():
            halo(ref, index + 2 * p, True, p).wait_recv()

        @pl.when(me < tiles - 1)
        def _():
            halo(ref, index + 2 * p + 1, False, p).wait_recv()

    def end_halo(ref, index, p):
        @pl.when(me < tiles - 1)
        def _():
            halo(ref, index + 2 * p, True, p).wait_send()

        @pl.when(me > 0)
        def _():
            halo(ref, index + 2 * p + 1, False, p).wait_send()

    def phase_copy(up):
        return pltpu.make_async_remote_copy(
            src_ref=ext.at[:, :, own : 2 * own, :],
            dst_ref=plo if up else phi,
            send_sem=ph_send.at[0 if up else 1],
            recv_sem=ph_recv.at[0 if up else 1],
            device_id={"phases": slab + 1 if up else slab - 1},
        )

    @pl.when(slab < slabs - 1)
    def _():
        phase_copy(True).start()

    @pl.when(slab > 0)
    def _():
        phase_copy(False).start()

    for p in range(phases):
        start_halo(ext, 0, p)

    def line_of(p, o, c):
        return line_ids[p, 0, c, o]

    def read_of(p, o, c):
        return read_ids[p, 0, c, o]

    def live_of(p, o, c):
        return jnp.where(c < counts[p, 0, o], 1.0, 0.0)

    pad = snd.shape[1] - slots * coils

    def fill(o, ref):
        ids = jnp.zeros((pad, 2 * seg), F32)
        row = iota((pad, 2 * seg), 0)
        for p in range(phases):
            for c in range(cap):
                s = p * cap + c
                value = image[p * lines + line_of(p, o, c)] * live_of(p, o, c)
                ref[o, s * coils : (s + 1) * coils, :] = value.astype(BF)
                ids = jnp.where(row == s, read_of(p, o, c).astype(F32), ids)
        ref[o, slots * coils :, :] = ids.astype(BF)

    def there(o):
        return pltpu.make_async_remote_copy(
            src_ref=snd.at[o],
            dst_ref=rcv.at[me],
            send_sem=a_send.at[o],
            recv_sem=a_recv.at[me],
            device_id={"tiles": o},
        )

    def arrived(t):
        return pltpu.make_async_remote_copy(
            src_ref=snd.at[t],
            dst_ref=rcv.at[t],
            send_sem=a_send.at[t],
            recv_sem=a_recv.at[t],
            device_id={"tiles": t},
        )

    def back(t):
        return pltpu.make_async_remote_copy(
            src_ref=back_snd.at[t],
            dst_ref=back_rcv.at[me],
            send_sem=b_send.at[t],
            recv_sem=b_recv.at[me],
            device_id={"tiles": t},
        )

    def returned(o):
        return pltpu.make_async_remote_copy(
            src_ref=back_snd.at[o],
            dst_ref=back_rcv.at[o],
            send_sem=b_send.at[o],
            recv_sem=b_recv.at[o],
            device_id={"tiles": o},
        )

    @pl.loop(1, tiles)
    def _(k):
        o = lax.rem(me + 1 + lax.rem(k + tiles // 2 - 2, tiles - 1), tiles)
        fill(o, snd)
        there(o).start()

    fill(me, rcv)

    build_matrices(taps_real, taps_imag, w_fwd, w_adj, planes)

    for p in range(phases):
        wait_halo(ext, 0, p)
        for y in range(rows_y):
            out = stencil(w_fwd[...], ext[p, y], own, False)
            for x in range(planes):
                rest = out[x * chan : (x + 1) * chan] - grid[p, x, y]
                grad[p, x, y] = -SPIRIT_WEIGHT * rest
                ext2[p, y, own + x * chan : own + (x + 1) * chan, :] = rest.astype(BF)
        start_halo(ext2, 2 * phases, p)

    for p in range(phases):
        for r in range(reads):
            racc[p, r] = -samples[p, r]

    def add_from(t):
        ids = rcv[t, slots * coils :, :].astype(F32)
        for p in range(phases):
            for c in range(cap):
                s = p * cap + c
                value = rcv[t, s * coils : (s + 1) * coils, :].astype(F32)
                own_id = jnp.broadcast_to(ids[s : s + 1], value.shape)
                for r in range(reads):
                    racc[p, r] = racc[p, r] + jnp.where(own_id == r, value, 0.0)

    add_from(me)

    @pl.loop(1, tiles)
    def _(k):
        t = lax.rem(me + tiles - k, tiles)
        arrived(t).wait_recv()
        add_from(t)

    for p in range(phases):
        for r in range(reads):
            value = racc[p, r]
            resid[p, r] = value
            racc[p, r] = value.astype(BF).astype(F32)

    def pick_for(t, ref):
        ids = rcv[t, slots * coils :, :].astype(F32)
        for p in range(phases):
            for c in range(cap):
                s = p * cap + c
                own_id = jnp.broadcast_to(ids[s : s + 1], (coils, 2 * seg))
                value = jnp.zeros((coils, 2 * seg), F32)
                for r in range(reads):
                    value = jnp.where(own_id == r, racc[p, r], value)
                ref[t, s * coils : (s + 1) * coils, :] = value.astype(BF)

    @pl.loop(1, tiles)
    def _(k):
        t = lax.rem(me + k, tiles)
        pick_for(t, back_snd)
        back(t).start()

    pick_for(me, back_rcv)

    @pl.when(slab > 0)
    def _():
        phase_copy(True).wait_recv()

    @pl.when(slab < slabs - 1)
    def _():
        phase_copy(False).wait_recv()

    below = jnp.where(slab > 0, 1.0, 0.0)
    above = jnp.where(slab < slabs - 1, 1.0, 0.0)
    for y in range(rows_y):
        for x in range(planes):
            part = slice(x * chan, (x + 1) * chan)
            field = [plo[phases - 2, y, part, :].astype(F32), plo[phases - 1, y, part, :].astype(F32)]
            field += [grid[p, x, y] for p in range(phases)]
            field += [phi[0, y, part, :].astype(F32), phi[1, y, part, :].astype(F32)]
            diff = [field[i] - 2.0 * field[i + 1] + field[i + 2] for i in range(phases + 2)]
            diff[0] = diff[0] * below
            diff[-1] = diff[-1] * above
            for p in range(phases):
                bend = diff[p] - 2.0 * diff[p + 1] + diff[p + 2]
                grad[p, x, y] = grad[p, x, y] + PHASE_WEIGHT * bend

    for p in range(phases):
        wait_halo(ext2, 2 * phases, p)
        for y in range(rows_y):
            out = stencil(w_adj[...], ext2[p, y], own, True)
            for x in range(planes):
                part = out[x * chan : (x + 1) * chan]
                grad[p, x, y] = grad[p, x, y] + SPIRIT_WEIGHT * part

    for i in range(phases * lines):
        lacc[i] = jnp.zeros((coils, 2 * seg), F32)

    def spread_from(o):
        for p in range(phases):
            for c in range(cap):
                s = p * cap + c
                value = back_rcv[o, s * coils : (s + 1) * coils, :].astype(F32) * live_of(p, o, c)
                line = line_of(p, o, c)
                for l in range(lines):
                    weight = jnp.where(line == l, 1.0, 0.0)
                    lacc[p * lines + l] = lacc[p * lines + l] + value * weight

    spread_from(me)

    @pl.loop(1, tiles)
    def _(k):
        o = lax.rem(me + tiles - k, tiles)
        returned(o).wait_recv()
        spread_from(o)

    lane = iota((coils, 2 * seg), 1)
    for p in range(phases):
        w = interp[p, 0]
        four = jnp.concatenate([w, w, w, w], axis=0)
        for l in range(lines):
            x, y = l // rows_y, l % rows_y
            total = lacc[p * lines + l]
            high = total.astype(BF).astype(F32)
            rest = total - high
            even = [jnp.where(lane < seg, v, 0.0) for v in (high, rest)]
            odd = [jnp.where(lane < seg, 0.0, v) for v in (high, rest)]
            both = jnp.concatenate(
                [jnp.concatenate(even, axis=1), jnp.concatenate(odd, axis=1)], axis=0
            ).astype(BF)
            woven = dot(weave, both).astype(BF)
            grad[p, x, y] = grad[p, x, y] + dot(woven, four)

    for p in range(phases):
        end_halo(ext, 0, p)
        end_halo(ext2, 2 * phases, p)

    @pl.when(slab < slabs - 1)
    def _():
        phase_copy(True).wait_send()

    @pl.when(slab > 0)
    def _():
        phase_copy(False).wait_send()

    @pl.loop(1, tiles)
    def _(k):
        o = lax.rem(me + k, tiles)
        there(o).wait_send()
        back(o).wait_send()


def on_device(
    slabs,
    tiles,
    kspace_grid,
    samples,
    interp_matrix,
    kernel_real,
    kernel_imag,
    segment_line,
    segment_readout,
    segment_count,
):
    phases, planes, rows_y, chan, depth = kspace_grid.shape
    kx, kz, coils, _ = kernel_real.shape
    cap = segment_line.shape[3]
    reads = samples.shape[1]
    seg = interp_matrix.shape[2]
    own = planes * chan
    slots = phases * cap
    message = slots * coils + 16 * -(-slots // 16)
    lines = planes * rows_y
    width = (planes + kx - 1) * chan
    dims = (slabs, tiles, phases, planes, rows_y, chan, depth, kx, kz, cap, reads)
    vmem = pl.BlockSpec(memory_space=pltpu.VMEM)
    dma = pltpu.SemaphoreType.DMA
    return pl.pallas_call(
        functools.partial(kernel, dims),
        out_shape=(
            jax.ShapeDtypeStruct(kspace_grid.shape, F32),
            jax.ShapeDtypeStruct(samples.shape, F32),
        ),
        in_specs=[pl.BlockSpec(memory_space=pltpu.SMEM)] * 3 + [pl.BlockSpec(memory_space=pltpu.HBM)] * 5,
        out_specs=(vmem, vmem),
        scratch_shapes=[
            pltpu.VMEM((phases, rows_y, 3 * own, depth), BF),
            pltpu.VMEM((phases, rows_y, 3 * own, depth), BF),
            pltpu.VMEM((phases, rows_y, own, depth), BF),
            pltpu.VMEM((phases, rows_y, own, depth), BF),
            pltpu.VMEM((phases * lines, coils, 2 * seg), F32),
            pltpu.VMEM((tiles, message, 2 * seg), BF),
            pltpu.VMEM((tiles, message, 2 * seg), BF),
            pltpu.VMEM((tiles, slots * coils, 2 * seg), BF),
            pltpu.VMEM((tiles, slots * coils, 2 * seg), BF),
            pltpu.VMEM((phases, reads, coils, 2 * seg), F32),
            pltpu.VMEM((phases * lines, coils, 2 * seg), F32),
            pltpu.VMEM((kz * own, width), BF),
            pltpu.VMEM((kz * own, width), BF),
            dma((4 * phases,)),
            dma((4 * phases,)),
            dma((2,)),
            dma((2,)),
            dma((tiles,)),
            dma((tiles,)),
            dma((tiles,)),
            dma((tiles,)),
            pltpu.VMEM(kspace_grid.shape, F32),
            pltpu.VMEM(samples.shape, F32),
            pltpu.VMEM(interp_matrix.shape, BF),
            pltpu.VMEM(kernel_real.shape, BF),
            pltpu.VMEM(kernel_imag.shape, BF),
            dma((5,)),
        ],
        compiler_params=pltpu.CompilerParams(
            collective_id=0, has_side_effects=True, vmem_limit_bytes=58 * 1024 * 1024
        ),
    )(
        jnp.transpose(segment_line, (0, 1, 3, 2)),
        jnp.transpose(segment_readout, (0, 1, 3, 2)),
        segment_count,
        kspace_grid,
        samples,
        interp_matrix,
        kernel_real,
        kernel_imag,
    )


def solution(mesh):
    return jax.shard_map(
        functools.partial(on_device, mesh.shape["phases"], mesh.shape["tiles"]),
        mesh=mesh,
        in_specs=(
            P("phases", "tiles", None, None, None),
            P("phases", "tiles", None, None),
            P("phases", "tiles", None, None),
            P(),
            P(),
            P("phases", "tiles", None, None),
            P("phases", "tiles", None, None),
            P("phases", "tiles", None),
        ),
        out_specs=(P("phases", "tiles", None, None, None), P("phases", "tiles", None, None)),
        check_vma=False,
    )
```
